512 devices in a mesh: clus: 128 (over z, x, core), src: 4 (over y).
Axes of the slice: x: 4, y: 4, z: 16, core: 2. Of those that a mesh axis runs over, the one named last changes fastest.
Arguments:
- embeddings: float32 [65536, 768], P(('clus', 'src'))
- cluster: int32 [65536], P(('clus', 'src')), may hold values from 0 to 1023, as said below
Outputs:
- centroids: float32 [1024, 768], P('clus')
- nearest: float32 [65536], P(('clus', 'src'))
The draws below stay inside these ranges and needn't reach their ends.
Inputs may be any that keep to these rules, and one draw needn't show every extreme that they name: Of one device's 128 rows, at most 2 have clusters of one owner (cluster // 8); one owner receives exactly 2 rows from every device.
All inputs are finite; a program needn't handle non-finite values.
Results may differ from the reference program's by a relative error of at most 0.00032.
Values may be sent and summed in bfloat16 or wider, within the bound.
No kernel may reach another device: no remote copies, remote signals or barrier semaphores. Data moves between devices by JAX's collectives and lax.ppermute only.
A program may use at most 64 MiB of HBM per device.

```python
import math
import jax
import jax.numpy as jnp
from jax import lax

D = 768
CLUS_DEV = 8
R_DEV = 128
CAP = 2
K = 1024
ROWS = 65536
N_CLUS = 128
N_SRC = 4
DEVICES = 512


def owners_drawn(key):
    hottest = jax.random.randint(jax.random.fold_in(key, 11), (), 0, N_CLUS)
    block_keys = jax.random.split(jax.random.fold_in(key, 12), DEVICES)

    def one_block(block_key):
        first_key, second_key = jax.random.split(block_key)
        picked = jax.random.permutation(first_key, (N_CLUS - 1) * CAP)[:R_DEV - CAP]
        others = picked // CAP
        others = others + (others >= hottest).astype(others.dtype)
        owners = jnp.concatenate([jnp.full((CAP,), hottest, jnp.int32), others.astype(jnp.int32)])
        return owners[jax.random.permutation(second_key, R_DEV)]
    return jax.vmap(one_block)(block_keys).reshape(-1)


def clusters_drawn(key):
    owners = owners_drawn(key)
    within = jax.random.randint(jax.random.fold_in(key, 13), (ROWS,), 0, CLUS_DEV)
    return (owners * CLUS_DEV + within).astype(jnp.int32)


def draw_cluster(key, part):
    return clusters_drawn(key)


def draw_embeddings(key, part):
    labels = clusters_drawn(key)
    key = jax.random.fold_in(key, 3)
    base_key, scale_key, sign_key, noise_key = jax.random.split(key, 4)
    centers = jax.random.normal(base_key, (K, D), jnp.float32)
    strength = jnp.exp(jax.random.uniform(scale_key, (ROWS, 1), jnp.float32, math.log(0.2), math.log(3.0)))
    signs = (2 * jax.random.randint(sign_key, (ROWS, 1), 0, 2) - 1).astype(jnp.float32)
    noise = jax.random.normal(noise_key, (ROWS, D), jnp.float32)
    return (signs * strength * centers[labels] + noise).astype(jnp.float32)


def setup_inputs(seed: int = 0) -> dict:
    streams_of = jax.random.split(jax.random.key(seed), 3)
    embeddings = draw_embeddings(jax.random.fold_in(streams_of[2], 71), 0)
    cluster = draw_cluster(jax.random.fold_in(streams_of[2], 71), 0)
    return {"embeddings": embeddings, "cluster": cluster}


def reference(embeddings, cluster):
    sums = jax.ops.segment_sum(embeddings, cluster, num_segments=K)
    centroids = sums * lax.rsqrt(lax.optimization_barrier(jnp.sum(sums * sums, axis=1, keepdims=True)) + 1e-06)
    unit = (embeddings * lax.rsqrt(lax.optimization_barrier(jnp.sum(embeddings * embeddings, axis=1, keepdims=True)) + 1e-06)).astype(jnp.bfloat16)
    owner = (cluster // CLUS_DEV).astype(jnp.int32)
    order = jnp.argsort(owner, stable=True).astype(jnp.int32)
    counts = jax.ops.segment_sum(jnp.ones_like(owner), owner, num_segments=N_CLUS)
    starts = (jnp.cumsum(counts) - counts).astype(jnp.int32)
    window = N_SRC * N_CLUS * CAP
    padded_unit = jnp.concatenate([unit[order], jnp.zeros((window, D), jnp.bfloat16)], axis=0)
    padded_ids = jnp.concatenate([cluster[order], jnp.full((window,), -1, jnp.int32)], axis=0)

    def per_owner(index):
        first = starts[index]
        member_rows = lax.dynamic_slice(padded_unit, (first, jnp.zeros((), jnp.int32)), (window, D)).astype(jnp.float32)
        member_ids = lax.dynamic_slice(padded_ids, (first,), (window,))
        places = jnp.arange(window, dtype=jnp.int32)
        member_ids = jnp.where(places < counts[index], member_ids, -1)
        scores = jnp.dot(member_rows, member_rows.T, precision=lax.Precision.HIGHEST, preferred_element_type=jnp.float32)
        allowed = (member_ids[:, None] == member_ids[None, :]) & (places[:, None] != places[None, :]) & (member_ids[:, None] >= 0)
        return lax.optimization_barrier(jnp.max(jnp.where(allowed, scores, jnp.float32(-1.0)), axis=1))
    maxima = lax.map(per_owner, jnp.arange(N_CLUS, dtype=jnp.int32))
    sorted_owner = owner[order]
    local_place = jnp.arange(ROWS, dtype=jnp.int32) - starts[sorted_owner]
    values = maxima[sorted_owner, local_place]
    nearest = jnp.zeros((ROWS,), jnp.float32).at[order].set(values)
    return (centroids, nearest)
```

```python
import jax
import jax.numpy as jnp
from jax import lax
from jax.experimental import pallas as pl
from jax.experimental.pallas import tpu as pltpu
from jax.sharding import PartitionSpec as P

CLUS_DEV = 8
OWNERS = 128
ROWS = 128
DIM = 768
WIDE = DIM + 128
EXTRA = 32
F32_EDGE = 3.38e38
VMEM = pltpu.CompilerParams(vmem_limit_bytes=48 * 1024 * 1024)


def pieces(value):
    high = jnp.clip(value, -F32_EDGE, F32_EDGE).astype(jnp.bfloat16)
    rest = value - high.astype(jnp.float32)
    middle = rest.astype(jnp.bfloat16)
    low = (rest - middle.astype(jnp.float32)).astype(jnp.bfloat16)
    return high, middle, low


def product(left, right, contract):
    return lax.dot_general(
        left, right, (contract, ((), ())), preferred_element_type=jnp.float32
    )


def place_kernel(rows_ref, cluster_ref, out_ref, code_ref):
    cluster = cluster_ref[...]
    owner = cluster // CLUS_DEV
    label = (cluster - owner * CLUS_DEV + 1).astype(jnp.float32)
    first = lax.broadcasted_iota(jnp.int32, (OWNERS, ROWS), 0)
    second = lax.broadcasted_iota(jnp.int32, (OWNERS, ROWS), 1)
    hits = first == owner
    earlier = product(
        hits.astype(jnp.bfloat16), (first < second).astype(jnp.bfloat16), ((1,), (0,))
    )
    split = pieces(rows_ref[...])
    for slot in range(2):
        chosen = jnp.where(hits & ((earlier > 0.5) == (slot == 1)), 1.0, 0.0)
        if slot == 1:
            code_ref[...] = owner * 2 + jnp.sum(chosen, axis=0, keepdims=True).astype(jnp.int32)
        mask = chosen.astype(jnp.bfloat16)
        placed = [product(mask, piece, ((1,), (0,))) for piece in split]
        out_ref[:, slot, :DIM] = (placed[0] + placed[1]) + placed[2]
        out_ref[:, slot, DIM:] = jnp.broadcast_to(
            jnp.sum(chosen * label, axis=1, keepdims=True), (OWNERS, 128)
        )


def unit_kernel(received_ref, packed_ref, label_ref):
    sums = jnp.zeros((128, DIM), jnp.float32)
    lane = lax.broadcasted_iota(jnp.int32, (OWNERS, 128), 1).astype(jnp.float32)
    weight = lax.broadcasted_iota(jnp.int32, (8, 128), 1).astype(jnp.float32) + 1.0
    rows_of_labels = []
    for slot in range(2):
        rows = received_ref[:, slot, :DIM]
        label = received_ref[:, slot, DIM:]
        here = slice(slot * OWNERS, (slot + 1) * OWNERS)
        label_ref[here, :] = label
        scale = lax.rsqrt(jnp.sum(rows * rows, axis=1, keepdims=True) + 1e-06)
        packed_ref[here, :] = (rows * scale).astype(jnp.bfloat16)
        member = (label == lane + 1.0).astype(jnp.bfloat16)
        for piece in pieces(rows):
            sums = sums + product(member, piece, ((0,), (0,)))
        rows_of_labels.append(product(weight.astype(jnp.bfloat16), member, ((1,), (1,))))
    high, middle, low = pieces(sums[:CLUS_DEV])
    packed_ref[256:272, :] = jnp.concatenate(
        [high.astype(jnp.float32), middle.astype(jnp.float32)], axis=0
    ).astype(jnp.bfloat16)
    label_rows = jnp.concatenate(rows_of_labels + [jnp.zeros((8, DIM - 256), jnp.float32)], axis=1)
    packed_ref[272:288, :] = jnp.concatenate(
        [low.astype(jnp.float32), label_rows], axis=0
    ).astype(jnp.bfloat16)


def score_kernel(label_ref, own_ref, next_ref, last_ref, across_ref, best_ref, centroid_ref):
    label = label_ref[:, :1]
    own = own_ref[:256, :]
    not_self = lax.broadcasted_iota(jnp.int32, (256, 256), 0) != lax.broadcasted_iota(
        jnp.int32, (256, 256), 1
    )
    best = jnp.full((256, 256), -1.0, jnp.float32)
    parts = []
    for ref in (own_ref, next_ref, last_ref, across_ref):
        scores = product(own, ref[:256, :], ((1,), (1,)))
        tail = ref[272:288, :].astype(jnp.float32)
        allowed = label == tail[8:9, :256]
        if ref is own_ref:
            allowed = allowed & not_self
        best = jnp.maximum(best, jnp.where(allowed, scores, -1.0))
        head = ref[256:272, :].astype(jnp.float32)
        parts.append((head[:8] + head[8:]) + tail[:8])
    most = jnp.max(best, axis=1, keepdims=True)
    lane = lax.broadcasted_iota(jnp.int32, (OWNERS, 128), 1)
    best_ref[...] = jnp.where(lane < 64, most[:128], most[128:])
    sums = (parts[0] + parts[3]) + (parts[1] + parts[2])
    centroid_ref[...] = sums * lax.rsqrt(jnp.sum(sums * sums, axis=1, keepdims=True) + 1e-06)


def pick_kernel(returned_ref, code_ref, nearest_ref):
    code = code_ref[...]
    owner = code // 2
    first_slot = code == owner * 2
    values = jnp.where(first_slot, returned_ref[:, :1], returned_ref[:, 127:])
    mine = lax.broadcasted_iota(jnp.int32, (OWNERS, ROWS), 0) == owner
    nearest_ref[...] = jnp.sum(jnp.where(mine, values, 0.0), axis=0, keepdims=True)


def call(kernel, outs, *operands):
    spec = pl.BlockSpec(memory_space=pltpu.VMEM)
    many = isinstance(outs, list)
    return pl.pallas_call(
        kernel,
        out_shape=outs,
        in_specs=[spec] * len(operands),
        out_specs=[spec] * len(outs) if many else spec,
        compiler_params=VMEM,
    )(*operands)


def on_device(embeddings, cluster):
    shape = jax.ShapeDtypeStruct
    sent, code = call(
        place_kernel,
        [shape((OWNERS, 2, WIDE), jnp.float32), shape((1, ROWS), jnp.int32)],
        embeddings,
        cluster.reshape(1, ROWS),
    )
    received = lax.all_to_all(sent, "clus", split_axis=0, concat_axis=0, tiled=True)
    packed, label = call(
        unit_kernel,
        [shape((256 + EXTRA, DIM), jnp.bfloat16), shape((256, 128), jnp.float32)],
        received,
    )
    others = [
        lax.ppermute(packed, "src", [(i, (i + step) % 4) for i in range(4)]) for step in (3, 1, 2)
    ]
    best, centroids = call(
        score_kernel,
        [shape((OWNERS, 128), jnp.float32), shape((CLUS_DEV, DIM), jnp.float32)],
        label,
        packed,
        *others,
    )
    returned = lax.all_to_all(best, "clus", split_axis=0, concat_axis=0, tiled=True)
    nearest = call(pick_kernel, shape((1, ROWS), jnp.float32), returned, code)
    return centroids, nearest.reshape(ROWS)


def solution(mesh):
    return jax.shard_map(
        on_device,
        mesh=mesh,
        in_specs=(P(("clus", "src"), None), P(("clus", "src"))),
        out_specs=(P("clus", None), P(("clus", "src"))),
        check_vma=False,
    )
```

```python
import jax
import jax.numpy as jnp
from jax import lax
from jax.experimental import pallas as pl
from jax.experimental.pallas import tpu as pltpu
from jax.sharding import PartitionSpec as P

CLUS_DEV = 8
OWNERS = 128
ROWS = 128
SLOTS = 256
DIM = 768
WIDE = DIM + 128
EDGE = 3.38e38
VMEM = pltpu.CompilerParams(vmem_limit_bytes=48 * 1024 * 1024)


def narrow(value):
    return jnp.clip(value, -EDGE, EDGE).astype(jnp.bfloat16)


def pieces(value):
    high = narrow(value)
    rest = value - high.astype(jnp.float32)
    middle = rest.astype(jnp.bfloat16)
    low = (rest - middle.astype(jnp.float32)).astype(jnp.bfloat16)
    return high, middle, low


def product(left, right, contract):
    return lax.dot_general(
        left, right, (contract, ((), ())), preferred_element_type=jnp.float32
    )


def iota(shape, dimension):
    return lax.broadcasted_iota(jnp.int32, shape, dimension)


def place_kernel(rows_ref, cluster_ref, unit_ref, rest_ref, code_ref):
    cluster = cluster_ref[...]
    owner = cluster // CLUS_DEV
    label = cluster - owner * CLUS_DEV
    first = iota((OWNERS, ROWS), 0)
    second = iota((OWNERS, ROWS), 1)
    hits = first == owner
    earlier = product(
        hits.astype(jnp.bfloat16), (first < second).astype(jnp.bfloat16), ((1,), (0,))
    )
    position = jnp.sum(jnp.where(hits & (earlier > 0.5), 1, 0), axis=0, keepdims=True)
    code = owner * 2 + position
    code_ref[...] = code
    chosen = (iota((SLOTS, ROWS), 0) == code).astype(jnp.bfloat16)

    rows = rows_ref[...]
    square = jnp.sum(rows * rows, axis=1, keepdims=True) + 1e-06
    scale = lax.rsqrt(square)
    norm = jnp.where(square < EDGE, square * scale, 0.0)
    unit = (rows * scale).astype(jnp.bfloat16)
    rest = narrow(rows - norm * unit.astype(jnp.float32))
    unit_ref[:, :DIM] = product(chosen, unit, ((1,), (0,))).astype(jnp.bfloat16)
    rest_ref[...] = product(chosen, rest, ((1,), (0,))).astype(jnp.bfloat16)

    high, middle, low = pieces(norm)
    norms = jnp.where(
        second == 8,
        high.astype(jnp.float32),
        jnp.where(
            second == 9,
            middle.astype(jnp.float32),
            jnp.where(second == 10, low.astype(jnp.float32), 0.0),
        ),
    ).astype(jnp.bfloat16)
    labels = (first == label).astype(jnp.bfloat16)
    unit_ref[:, DIM:] = (
        product(chosen, norms, ((1,), (0,))) + product(chosen, labels, ((1,), (1,)))
    ).astype(jnp.bfloat16)


def member_of(ref):
    tail = ref[:, DIM:]
    return jnp.where(iota((SLOTS, 128), 1) < CLUS_DEV, tail, jnp.zeros_like(tail))


def score_kernel(own_ref, next_ref, last_ref, across_ref, best_ref):
    own = own_ref[:, :DIM]
    own_member = member_of(own_ref)
    not_self = iota((SLOTS, SLOTS), 0) != iota((SLOTS, SLOTS), 1)
    best = jnp.full((SLOTS, SLOTS), -1.0, jnp.float32)
    for ref in (own_ref, next_ref, last_ref, across_ref):
        scores = product(own, ref[:, :DIM], ((1,), (1,)))
        allowed = product(own_member, member_of(ref), ((1,), (1,))) > 0.5
        if ref is own_ref:
            allowed = allowed & not_self
        best = jnp.maximum(best, jnp.where(allowed, scores, -1.0))
    most = jnp.max(best, axis=1, keepdims=True)
    slot, lane = iota((SLOTS, 128), 0), iota((SLOTS, 128), 1)
    spread = jnp.where((lane < 64) == (slot % 2 == 0), most, 0.0)
    pair = (iota((OWNERS, SLOTS), 1) // 2 == iota((OWNERS, SLOTS), 0)).astype(jnp.bfloat16)
    high, middle, low = [product(pair, piece, ((1,), (0,))) for piece in pieces(spread)]
    best_ref[...] = (high + middle) + low


def sum_kernel(unit_ref, rest_ref, sum_ref):
    tail = unit_ref[:, DIM:].astype(jnp.float32)
    norm = (tail[:, 8:9] + tail[:, 9:10]) + tail[:, 10:11]
    member = member_of(unit_ref)
    sums = product(member, rest_ref[...], ((0,), (0,)))
    for piece in pieces(member.astype(jnp.float32) * norm):
        sums = sums + product(piece, unit_ref[:, :DIM], ((0,), (0,)))
    sum_ref[...] = sums[:CLUS_DEV]


def centroid_kernel(parts_ref, centroid_ref):
    sums = (parts_ref[:8] + parts_ref[8:16]) + (parts_ref[16:24] + parts_ref[24:])
    centroid_ref[...] = sums * lax.rsqrt(jnp.sum(sums * sums, axis=1, keepdims=True) + 1e-06)


def pick_kernel(returned_ref, code_ref, nearest_ref):
    code = code_ref[...]
    owner = code // 2
    first_slot = code == owner * 2
    values = jnp.where(first_slot, returned_ref[:, :1], returned_ref[:, 127:])
    mine = iota((OWNERS, ROWS), 0) == owner
    nearest_ref[...] = jnp.sum(jnp.where(mine, values, 0.0), axis=0, keepdims=True)


def call(kernel, outs, *operands):
    spec = pl.BlockSpec(memory_space=pltpu.VMEM)
    many = isinstance(outs, list)
    return pl.pallas_call(
        kernel,
        out_shape=outs,
        in_specs=[spec] * len(operands),
        out_specs=[spec] * len(outs) if many else spec,
        compiler_params=VMEM,
    )(*operands)


def exchange(value):
    return lax.all_to_all(value, "clus", split_axis=0, concat_axis=0, tiled=True)


def on_device(embeddings, cluster):
    shape = jax.ShapeDtypeStruct
    unit, rest, code = call(
        place_kernel,
        [
            shape((SLOTS, WIDE), jnp.bfloat16),
            shape((SLOTS, DIM), jnp.bfloat16),
            shape((1, ROWS), jnp.int32),
        ],
        embeddings,
        cluster.reshape(1, ROWS),
    )
    unit = exchange(unit)
    rest = exchange(rest)
    others = [
        lax.ppermute(unit, "src", [(i, (i + step) % 4) for i in range(4)]) for step in (3, 1, 2)
    ]
    best = call(score_kernel, shape((OWNERS, 128), jnp.float32), unit, *others)
    returned = exchange(best)
    partial = call(sum_kernel, shape((CLUS_DEV, DIM), jnp.float32), unit, rest)
    parts = lax.all_gather(partial, "src", axis=0, tiled=True)
    centroids = call(centroid_kernel, shape((CLUS_DEV, DIM), jnp.float32), parts)
    nearest = call(pick_kernel, shape((1, ROWS), jnp.float32), returned, code)
    return centroids, nearest.reshape(ROWS)


def solution(mesh):
    return jax.shard_map(
        on_device,
        mesh=mesh,
        in_specs=(P(("clus", "src"), None), P(("clus", "src"))),
        out_specs=(P("clus", None), P(("clus", "src"))),
        check_vma=False,
    )
```

```python
import jax
import jax.numpy as jnp
from jax import lax
from jax.experimental import pallas as pl
from jax.experimental.pallas import tpu as pltpu
from jax.sharding import PartitionSpec as P

CLUS_DEV = 8
OWNERS = 128
ROWS = 128
SLOTS = 256
DIM = 768
WIDE = DIM + 128
GROUPS = DIM // 128
LEAST_POWER = -3520.0
EDGE = 3.38e38
VMEM = pltpu.CompilerParams(vmem_limit_bytes=48 * 1024 * 1024)


def narrow(value):
    return jnp.clip(value, -EDGE, EDGE).astype(jnp.bfloat16)


def pieces(value):
    high = narrow(value)
    rest = value - high.astype(jnp.float32)
    middle = rest.astype(jnp.bfloat16)
    low = (rest - middle.astype(jnp.float32)).astype(jnp.bfloat16)
    return high, middle, low


def product(left, right, contract):
    return lax.dot_general(
        left, right, (contract, ((), ())), preferred_element_type=jnp.float32
    )


def iota(shape, dimension):
    return lax.broadcasted_iota(jnp.int32, shape, dimension)


def stored(high, low):
    return (high * 256.0 + low).astype(jnp.int32).astype(jnp.int16)


def place_kernel(rows_ref, cluster_ref, sent_ref, code_ref):
    cluster = cluster_ref[...]
    owner = cluster // CLUS_DEV
    label = cluster - owner * CLUS_DEV
    first = iota((OWNERS, ROWS), 0)
    second = iota((OWNERS, ROWS), 1)
    hits = first == owner
    earlier = product(
        hits.astype(jnp.bfloat16), (first < second).astype(jnp.bfloat16), ((1,), (0,))
    )
    position = jnp.sum(jnp.where(hits & (earlier > 0.5), 1, 0), axis=0, keepdims=True)
    code = owner * 2 + position
    code_ref[...] = code
    chosen = (iota((SLOTS, ROWS), 0) == code).astype(jnp.bfloat16)

    def placed(steps):
        high = jnp.floor(steps * (1.0 / 256.0) + 0.5)
        low = steps - high * 256.0
        return (
            product(chosen, high.astype(jnp.bfloat16), ((1,), (0,))),
            product(chosen, low.astype(jnp.bfloat16), ((1,), (0,))),
        )

    powers = jnp.zeros((ROWS, 128), jnp.float32)
    for group in range(GROUPS):
        here = slice(group * 128, (group + 1) * 128)
        values = rows_ref[:, here]
        most = jnp.max(jnp.abs(values), axis=1, keepdims=True)
        power = jnp.clip(jnp.ceil(jnp.log2(most) * 32.0), LEAST_POWER, 4096.0)
        steps = jnp.round(values * jnp.exp2(15.0 - power * (1.0 / 32.0)))
        sent_ref[:, here] = stored(*placed(jnp.clip(steps, -32767.0, 32767.0)))
        powers = jnp.where(second == CLUS_DEV + group, power, powers)
    labels = (first == label).astype(jnp.bfloat16)
    high, low = placed(powers)
    sent_ref[:, DIM:] = stored(high, low + product(chosen, labels, ((1,), (1,))))


def decoded(ref):
    tail = ref[:, DIM:].astype(jnp.float32)
    member = jnp.where(iota((SLOTS, 128), 1) < CLUS_DEV, tail, 0.0).astype(jnp.bfloat16)
    step = jnp.exp2(tail * (1.0 / 32.0) - 15.0)
    rows = [
        ref[:, group * 128 : (group + 1) * 128].astype(jnp.float32)
        * step[:, CLUS_DEV + group : CLUS_DEV + group + 1]
        for group in range(GROUPS)
    ]
    return member, rows


def unit_of(rows):
    square = rows[0] * rows[0]
    for values in rows[1:]:
        square = square + values * values
    scale = lax.rsqrt(jnp.sum(square, axis=1, keepdims=True) + 1e-06)
    return jnp.concatenate([(values * scale).astype(jnp.bfloat16) for values in rows], axis=1)


def score_kernel(own_ref, next_ref, last_ref, across_ref, best_ref):
    not_self = iota((SLOTS, SLOTS), 0) != iota((SLOTS, SLOTS), 1)
    best = jnp.full((SLOTS, SLOTS), -1.0, jnp.float32)
    for ref in (own_ref, next_ref, last_ref, across_ref):
        member, rows = decoded(ref)
        unit = unit_of(rows)
        if ref is own_ref:
            own, own_member = unit, member
        scores = product(own, unit, ((1,), (1,)))
        allowed = product(own_member, member, ((1,), (1,))) > 0.5
        if ref is own_ref:
            allowed = allowed & not_self
        best = jnp.maximum(best, jnp.where(allowed, scores, -1.0))
    most = jnp.max(best, axis=1, keepdims=True)
    slot, lane = iota((SLOTS, 128), 0), iota((SLOTS, 128), 1)
    spread = jnp.where((lane < 64) == (slot % 2 == 0), most, 0.0)
    pair = (iota((OWNERS, SLOTS), 1) // 2 == iota((OWNERS, SLOTS), 0)).astype(jnp.bfloat16)
    high, middle, low = [product(pair, piece, ((1,), (0,))) for piece in pieces(spread)]
    best_ref[...] = (high + middle) + low


def centroid_kernel(own_ref, next_ref, last_ref, across_ref, centroid_ref):
    parts = []
    for ref in (own_ref, next_ref, last_ref, across_ref):
        member, rows = decoded(ref)
        high, middle, low = [
            product(member, piece, ((0,), (0,)))[:CLUS_DEV]
            for piece in pieces(jnp.concatenate(rows, axis=1))
        ]
        parts.append((high + middle) + low)
    sums = (parts[0] + parts[3]) + (parts[1] + parts[2])
    centroid_ref[...] = sums * lax.rsqrt(jnp.sum(sums * sums, axis=1, keepdims=True) + 1e-06)


def pick_kernel(returned_ref, code_ref, nearest_ref):
    code = code_ref[...]
    owner = code // 2
    first_slot = code == owner * 2
    values = jnp.where(first_slot, returned_ref[:, :1], returned_ref[:, 127:])
    mine = iota((OWNERS, ROWS), 0) == owner
    nearest_ref[...] = jnp.sum(jnp.where(mine, values, 0.0), axis=0, keepdims=True)


def call(kernel, outs, *operands):
    spec = pl.BlockSpec(memory_space=pltpu.VMEM)
    many = isinstance(outs, list)
    return pl.pallas_call(
        kernel,
        out_shape=outs,
        in_specs=[spec] * len(operands),
        out_specs=[spec] * len(outs) if many else spec,
        compiler_params=VMEM,
    )(*operands)


def exchange(value):
    return lax.all_to_all(value, "clus", split_axis=0, concat_axis=0, tiled=True)


def on_device(embeddings, cluster):
    shape = jax.ShapeDtypeStruct
    sent, code = call(
        place_kernel,
        [shape((SLOTS, WIDE), jnp.int16), shape((1, ROWS), jnp.int32)],
        embeddings,
        cluster.reshape(1, ROWS),
    )
    block = exchange(sent)
    blocks = [block] + [
        lax.ppermute(block, "src", [(i, (i + step) % 4) for i in range(4)]) for step in (3, 1, 2)
    ]
    best = call(score_kernel, shape((OWNERS, 128), jnp.float32), *blocks)
    returned = exchange(best)
    centroids = call(centroid_kernel, shape((CLUS_DEV, DIM), jnp.float32), *blocks)
    nearest = call(pick_kernel, shape((1, ROWS), jnp.float32), returned, code)
    return centroids, nearest.reshape(ROWS)


def solution(mesh):
    return jax.shard_map(
        on_device,
        mesh=mesh,
        in_specs=(P(("clus", "src"), None), P(("clus", "src"))),
        out_specs=(P("clus", None), P(("clus", "src"))),
        check_vma=False,
    )
```

```python
import jax
import jax.numpy as jnp
from jax import lax
from jax.experimental import pallas as pl
from jax.experimental.pallas import tpu as pltpu
from jax.sharding import PartitionSpec as P

CLUS_DEV = 8
OWNERS = 128
ROWS = 128
SLOTS = 256
DIM = 768
WIDE = DIM + 128
GROUPS = DIM // 128
LEAST_POWER = -3520.0
EDGE = 3.38e38
VMEM = pltpu.CompilerParams(vmem_limit_bytes=48 * 1024 * 1024)


def narrow(value):
    return jnp.clip(value, -EDGE, EDGE).astype(jnp.bfloat16)


def pieces(value):
    high = narrow(value)
    rest = value - high.astype(jnp.float32)
    middle = rest.astype(jnp.bfloat16)
    low = (rest - middle.astype(jnp.float32)).astype(jnp.bfloat16)
    return high, middle, low


def product(left, right, contract):
    return lax.dot_general(
        left, right, (contract, ((), ())), preferred_element_type=jnp.float32
    )


def iota(shape, dimension):
    return lax.broadcasted_iota(jnp.int32, shape, dimension)


def stored(high, low):
    return (high * 256.0 + low).astype(jnp.int32).astype(jnp.int16)


def place_kernel(rows_ref, cluster_ref, sent_ref, code_ref):
    cluster = cluster_ref[...]
    owner = cluster // CLUS_DEV
    label = cluster - owner * CLUS_DEV
    first = iota((OWNERS, ROWS), 0)
    second = iota((OWNERS, ROWS), 1)
    hits = first == owner
    earlier = product(
        hits.astype(jnp.bfloat16), (first < second).astype(jnp.bfloat16), ((1,), (0,))
    )
    position = jnp.sum(jnp.where(hits & (earlier > 0.5), 1, 0), axis=0, keepdims=True)
    code = owner * 2 + position
    code_ref[...] = code
    chosen = (iota((SLOTS, ROWS), 0) == code).astype(jnp.bfloat16)

    def placed(steps):
        high = jnp.floor(steps * (1.0 / 256.0) + 0.5)
        low = steps - high * 256.0
        return (
            product(chosen, high.astype(jnp.bfloat16), ((1,), (0,))),
            product(chosen, low.astype(jnp.bfloat16), ((1,), (0,))),
        )

    powers = jnp.zeros((ROWS, 128), jnp.float32)
    for group in range(GROUPS):
        here = slice(group * 128, (group + 1) * 128)
        values = rows_ref[:, here]
        most = jnp.max(jnp.abs(values), axis=1, keepdims=True)
        power = jnp.clip(jnp.ceil(jnp.log2(most) * 32.0), LEAST_POWER, 4096.0)
        steps = jnp.round(values * jnp.exp2(15.0 - power * (1.0 / 32.0)))
        sent_ref[:, here] = stored(*placed(jnp.clip(steps, -32767.0, 32767.0)))
        powers = jnp.where(second == CLUS_DEV + group, power, powers)
    labels = (first == label).astype(jnp.bfloat16)
    high, low = placed(powers)
    sent_ref[:, DIM:] = stored(high, low + product(chosen, labels, ((1,), (1,))))


def decoded(ref, start):
    here = slice(start, start + SLOTS)
    tail = ref[here, DIM:].astype(jnp.float32)
    member = jnp.where(iota((SLOTS, 128), 1) < CLUS_DEV, tail, 0.0).astype(jnp.bfloat16)
    step = jnp.exp2(tail * (1.0 / 32.0) - 15.0)
    rows = [
        ref[here, group * 128 : (group + 1) * 128].astype(jnp.float32)
        * step[:, CLUS_DEV + group : CLUS_DEV + group + 1]
        for group in range(GROUPS)
    ]
    return member, rows


def score_kernel(all_ref, best_ref, unit_ref, member_ref):
    starts = range(0, all_ref.shape[0], SLOTS)
    for start in starts:
        member, rows = decoded(all_ref, start)
        square = rows[0] * rows[0]
        for values in rows[1:]:
            square = square + values * values
        scale = lax.rsqrt(jnp.sum(square, axis=1, keepdims=True) + 1e-06)
        here = slice(start, start + SLOTS)
        for group, values in enumerate(rows):
            unit_ref[here, group * 128 : (group + 1) * 128] = (values * scale).astype(jnp.bfloat16)
        member_ref[here, :] = member
    offset = pl.multiple_of(lax.axis_index("src") * SLOTS, SLOTS)
    own = unit_ref[pl.ds(offset, SLOTS), :]
    own_member = member_ref[pl.ds(offset, SLOTS), :]
    apart = iota((SLOTS, SLOTS), 0) - iota((SLOTS, SLOTS), 1) + offset
    best = jnp.full((SLOTS, SLOTS), -1.0, jnp.float32)
    for start in starts:
        here = slice(start, start + SLOTS)
        scores = product(own, unit_ref[here, :], ((1,), (1,)))
        same = product(own_member, member_ref[here, :], ((1,), (1,))) > 0.5
        best = jnp.maximum(best, jnp.where(same & (apart != start), scores, -1.0))
    most = jnp.max(best, axis=1, keepdims=True)
    slot, lane = iota((SLOTS, 128), 0), iota((SLOTS, 128), 1)
    spread = jnp.where((lane < 64) == (slot % 2 == 0), most, 0.0)
    pair = (iota((OWNERS, SLOTS), 1) // 2 == iota((OWNERS, SLOTS), 0)).astype(jnp.bfloat16)
    high, middle, low = [product(pair, piece, ((1,), (0,))) for piece in pieces(spread)]
    best_ref[...] = (high + middle) + low


def centroid_kernel(all_ref, centroid_ref):
    sums = jnp.zeros((CLUS_DEV, DIM), jnp.float32)
    for start in range(0, all_ref.shape[0], SLOTS):
        member, rows = decoded(all_ref, start)
        for piece in pieces(jnp.concatenate(rows, axis=1)):
            sums = sums + product(member, piece, ((0,), (0,)))[:CLUS_DEV]
    centroid_ref[...] = sums * lax.rsqrt(jnp.sum(sums * sums, axis=1, keepdims=True) + 1e-06)


def pick_kernel(returned_ref, code_ref, nearest_ref):
    code = code_ref[...]
    owner = code // 2
    first_slot = code == owner * 2
    values = jnp.where(first_slot, returned_ref[:, :1], returned_ref[:, 127:])
    mine = iota((OWNERS, ROWS), 0) == owner
    nearest_ref[...] = jnp.sum(jnp.where(mine, values, 0.0), axis=0, keepdims=True)


def call(kernel, outs, *operands, scratch=()):
    spec = pl.BlockSpec(memory_space=pltpu.VMEM)
    many = isinstance(outs, list)
    return pl.pallas_call(
        kernel,
        out_shape=outs,
        in_specs=[spec] * len(operands),
        out_specs=[spec] * len(outs) if many else spec,
        scratch_shapes=scratch,
        compiler_params=VMEM,
    )(*operands)


def exchange(value):
    return lax.all_to_all(value, "clus", split_axis=0, concat_axis=0, tiled=True)


def on_device(embeddings, cluster):
    shape = jax.ShapeDtypeStruct
    sent, code = call(
        place_kernel,
        [shape((SLOTS, WIDE), jnp.int16), shape((1, ROWS), jnp.int32)],
        embeddings,
        cluster.reshape(1, ROWS),
    )
    rows = lax.all_gather(exchange(sent), "src", axis=0, tiled=True)
    best = call(
        score_kernel,
        shape((OWNERS, 128), jnp.float32),
        rows,
        scratch=[
            pltpu.VMEM((rows.shape[0], DIM), jnp.bfloat16),
            pltpu.VMEM((rows.shape[0], 128), jnp.bfloat16),
        ],
    )
    returned = exchange(best)
    centroids = call(centroid_kernel, shape((CLUS_DEV, DIM), jnp.float32), rows)
    nearest = call(pick_kernel, shape((1, ROWS), jnp.float32), returned, code)
    return centroids, nearest.reshape(ROWS)


def solution(mesh):
    return jax.shard_map(
        on_device,
        mesh=mesh,
        in_specs=(P(("clus", "src"), None), P(("clus", "src"))),
        out_specs=(P("clus", None), P(("clus", "src"))),
        check_vma=False,
    )
```

```python
import jax
import jax.numpy as jnp
from jax import lax
from jax.experimental import pallas as pl
from jax.experimental.pallas import tpu as pltpu
from jax.sharding import PartitionSpec as P

CLUS_DEV = 8
OWNERS = 128
ROWS = 128
SLOTS = 256
DIM = 768
WIDE = DIM + 128
GROUPS = DIM // 128
HALF = 512
LEAST_POWER = -2560.0
COARSE = CLUS_DEV + GROUPS
POWER = COARSE + 2
FINE = 2.0**21
TINY = 1e-37
EDGE = 3.38e38
VMEM = pltpu.CompilerParams(vmem_limit_bytes=48 * 1024 * 1024)


def narrow(value):
    return jnp.clip(value, -EDGE, EDGE).astype(jnp.bfloat16)


def pieces(value):
    high = narrow(value)
    rest = value - high.astype(jnp.float32)
    middle = rest.astype(jnp.bfloat16)
    low = (rest - middle.astype(jnp.float32)).astype(jnp.bfloat16)
    return high, middle, low


def product(left, right, contract):
    return lax.dot_general(
        left, right, (contract, ((), ())), preferred_element_type=jnp.float32
    )


def iota(shape, dimension):
    return lax.broadcasted_iota(jnp.int32, shape, dimension)


def stored(high, low):
    return (high * 256.0 + low).astype(jnp.int32).astype(jnp.int16)


def place_kernel(rows_ref, cluster_ref, sent_ref, code_ref):
    cluster = cluster_ref[...]
    owner = cluster // CLUS_DEV
    label = cluster - owner * CLUS_DEV
    first = iota((OWNERS, ROWS), 0)
    second = iota((OWNERS, ROWS), 1)
    hits = first == owner
    earlier = product(
        hits.astype(jnp.bfloat16), (first < second).astype(jnp.bfloat16), ((1,), (0,))
    )
    position = jnp.sum(jnp.where(hits & (earlier > 0.5), 1, 0), axis=0, keepdims=True)
    code = owner * 2 + position
    code_ref[...] = code
    chosen = (iota((SLOTS, ROWS), 0) == code).astype(jnp.bfloat16)

    def placed(steps):
        high = jnp.floor(steps * (1.0 / 256.0) + 0.5)
        low = steps - high * 256.0
        return (
            product(chosen, high.astype(jnp.bfloat16), ((1,), (0,))),
            product(chosen, low.astype(jnp.bfloat16), ((1,), (0,))),
        )

    groups = [rows_ref[:, group * 128 : (group + 1) * 128] for group in range(GROUPS)]
    square = groups[0] * groups[0]
    for values in groups[1:]:
        square = square + values * values
    scale = lax.rsqrt(jnp.sum(square, axis=1, keepdims=True) + 1e-06)
    tops = [
        jnp.log2(jnp.maximum(jnp.max(jnp.abs(values), axis=1, keepdims=True), TINY))
        for values in groups
    ]
    top = tops[0]
    for other in tops[1:]:
        top = jnp.maximum(top, other)
    power = jnp.clip(jnp.ceil(top * 32.0), LEAST_POWER, 4096.0)
    top = power * (1.0 / 32.0)
    factor = jnp.where(scale > 0.0, top - 15.0 + jnp.log2(jnp.maximum(scale, TINY)), -250.0)
    coarse = jnp.round(factor * 128.0)
    fine = jnp.round((factor - coarse * (1.0 / 128.0)) * FINE)
    fields = jnp.where(second == POWER, power, 0.0)
    fields = jnp.where(second == COARSE, coarse, jnp.where(second == COARSE + 1, fine, fields))
    for group, values in enumerate(groups):
        below = jnp.clip(jnp.floor(top - tops[group]), 0.0, 30.0)
        steps = jnp.round(values * jnp.exp2(15.0 - top + below))
        here = slice(group * 128, (group + 1) * 128)
        sent_ref[:, here] = stored(*placed(jnp.clip(steps, -32767.0, 32767.0)))
        fields = jnp.where(second == CLUS_DEV + group, below, fields)
    labels = (first == label).astype(jnp.bfloat16)
    high, low = placed(fields)
    sent_ref[:, DIM:] = stored(high, low + product(chosen, labels, ((1,), (1,))))


def fields_of(ref, here):
    tail = ref[here, DIM:].astype(jnp.float32)
    lane = iota(tail.shape, 1)
    member = jnp.where(lane < CLUS_DEV, tail, 0.0).astype(jnp.bfloat16)
    group = (lane >= CLUS_DEV) & (lane < CLUS_DEV + GROUPS)
    below = jnp.where(group, jnp.exp2(-jnp.where(group, tail, 0.0)), 0.0).astype(jnp.bfloat16)
    spread = iota((128, DIM), 1) // 128 + CLUS_DEV == iota((128, DIM), 0)
    return tail, member, product(below, spread.astype(jnp.bfloat16), ((1,), (0,)))


def score_kernel(all_ref, best_ref, unit_ref, member_ref):
    for start in range(0, all_ref.shape[0], HALF):
        here = slice(start, start + HALF)
        tail, member, below = fields_of(all_ref, here)
        factor = jnp.exp2(
            tail[:, COARSE : COARSE + 1] * (1.0 / 128.0)
            + tail[:, COARSE + 1 : COARSE + 2] * (1.0 / FINE)
        )
        unit_ref[here, :] = (all_ref[here, :DIM].astype(jnp.float32) * (below * factor)).astype(
            jnp.bfloat16
        )
        member_ref[here, :] = member
    offset = pl.multiple_of(lax.axis_index("src") * SLOTS, SLOTS)
    own = unit_ref[pl.ds(offset, SLOTS), :]
    own_member = member_ref[pl.ds(offset, SLOTS), :]
    apart = iota((SLOTS, SLOTS), 1) - iota((SLOTS, SLOTS), 0) + offset
    best = jnp.full((SLOTS, SLOTS), -1.0, jnp.float32)
    for start in range(0, all_ref.shape[0], SLOTS):
        here = slice(start, start + SLOTS)
        scores = product(unit_ref[here, :], own, ((1,), (1,)))
        same = product(member_ref[here, :], own_member, ((1,), (1,))) > 0.5
        best = jnp.maximum(best, jnp.where(same & (apart != start), scores, -1.0))
    most = jnp.max(best, axis=0, keepdims=True)
    slot_of = iota((OWNERS, SLOTS), 1) - iota((OWNERS, SLOTS), 0) * 2
    first, second = [
        jnp.sum(jnp.where(slot_of == slot, most, 0.0), axis=1, keepdims=True) for slot in range(2)
    ]
    best_ref[...] = jnp.where(iota((OWNERS, 128), 1) < 64, first, second)


def centroid_kernel(all_ref, centroid_ref):
    sums = jnp.zeros((CLUS_DEV, DIM), jnp.float32)
    for start in range(0, all_ref.shape[0], SLOTS):
        here = slice(start, start + SLOTS)
        tail, member, below = fields_of(all_ref, here)
        step = jnp.exp2(tail[:, POWER : POWER + 1] * (1.0 / 32.0) - 15.0)
        rows = all_ref[here, :DIM].astype(jnp.float32) * (below * step)
        for piece in pieces(rows):
            sums = sums + product(member, piece, ((0,), (0,)))[:CLUS_DEV]
    centroid_ref[...] = sums * lax.rsqrt(jnp.sum(sums * sums, axis=1, keepdims=True) + 1e-06)


def pick_kernel(returned_ref, code_ref, nearest_ref):
    code = code_ref[...]
    owner = code // 2
    first_slot = code == owner * 2
    values = jnp.where(first_slot, returned_ref[:, :1], returned_ref[:, 127:])
    mine = iota((OWNERS, ROWS), 0) == owner
    nearest_ref[...] = jnp.sum(jnp.where(mine, values, 0.0), axis=0, keepdims=True)


def call(kernel, outs, *operands, scratch=()):
    spec = pl.BlockSpec(memory_space=pltpu.VMEM)
    many = isinstance(outs, list)
    return pl.pallas_call(
        kernel,
        out_shape=outs,
        in_specs=[spec] * len(operands),
        out_specs=[spec] * len(outs) if many else spec,
        scratch_shapes=scratch,
        compiler_params=VMEM,
    )(*operands)


def exchange(value):
    return lax.all_to_all(value, "clus", split_axis=0, concat_axis=0, tiled=True)


def on_device(embeddings, cluster):
    shape = jax.ShapeDtypeStruct
    sent, code = call(
        place_kernel,
        [shape((SLOTS, WIDE), jnp.int16), shape((1, ROWS), jnp.int32)],
        embeddings,
        cluster.reshape(1, ROWS),
    )
    rows = lax.all_gather(exchange(sent), "src", axis=0, tiled=True)
    best = call(
        score_kernel,
        shape((OWNERS, 128), jnp.float32),
        rows,
        scratch=[
            pltpu.VMEM((rows.shape[0], DIM), jnp.bfloat16),
            pltpu.VMEM((rows.shape[0], 128), jnp.bfloat16),
        ],
    )
    returned = exchange(best)
    centroids = call(centroid_kernel, shape((CLUS_DEV, DIM), jnp.float32), rows)
    nearest = call(pick_kernel, shape((1, ROWS), jnp.float32), returned, code)
    return centroids, nearest.reshape(ROWS)


def solution(mesh):
    return jax.shard_map(
        on_device,
        mesh=mesh,
        in_specs=(P(("clus", "src"), None), P(("clus", "src"))),
        out_specs=(P("clus", None), P(("clus", "src"))),
        check_vma=False,
    )
```

```python
import jax
import jax.numpy as jnp
from jax import lax
from jax.experimental import pallas as pl
from jax.experimental.pallas import tpu as pltpu
from jax.sharding import Mesh
from jax.sharding import PartitionSpec as P

CLUS_DEV = 8
AXES = {"z": 16, "x": 4, "core": 2, "yh": 2, "yl": 2}
OWNER_AXES = ("z", "x", "yh")
MEET_AXES = ("yl", "core")
OWNERS = 128
ROWS = 128
SLOTS = 256
DIM = 768
WIDE = DIM + 128
GROUPS = DIM // 128
HALF = 512
LEAST_POWER = -2560.0
COARSE = CLUS_DEV + GROUPS
POWER = COARSE + 2
FINE = 2.0**21
TINY = 1e-37
EDGE = 3.38e38
VMEM = pltpu.CompilerParams(vmem_limit_bytes=48 * 1024 * 1024)


def narrow(value):
    return jnp.clip(value, -EDGE, EDGE).astype(jnp.bfloat16)


def pieces(value):
    high = narrow(value)
    rest = value - high.astype(jnp.float32)
    middle = rest.astype(jnp.bfloat16)
    low = (rest - middle.astype(jnp.float32)).astype(jnp.bfloat16)
    return high, middle, low


def product(left, right, contract):
    return lax.dot_general(
        left, right, (contract, ((), ())), preferred_element_type=jnp.float32
    )


def iota(shape, dimension):
    return lax.broadcasted_iota(jnp.int32, shape, dimension)


def stored(high, low):
    return (high * 256.0 + low).astype(jnp.int32).astype(jnp.int16)


def place_kernel(rows_ref, cluster_ref, sent_ref, code_ref):
    cluster = cluster_ref[...]
    owner = cluster // CLUS_DEV
    label = cluster - owner * CLUS_DEV
    first = iota((OWNERS, ROWS), 0)
    second = iota((OWNERS, ROWS), 1)
    hits = first == owner
    earlier = product(
        hits.astype(jnp.bfloat16), (first < second).astype(jnp.bfloat16), ((1,), (0,))
    )
    position = jnp.sum(jnp.where(hits & (earlier > 0.5), 1, 0), axis=0, keepdims=True)
    code = owner * 2 + position
    code_ref[...] = code
    chosen = (iota((SLOTS, ROWS), 0) == code).astype(jnp.bfloat16)

    def placed(steps):
        high = jnp.floor(steps * (1.0 / 256.0) + 0.5)
        low = steps - high * 256.0
        return (
            product(chosen, high.astype(jnp.bfloat16), ((1,), (0,))),
            product(chosen, low.astype(jnp.bfloat16), ((1,), (0,))),
        )

    groups = [rows_ref[:, group * 128 : (group + 1) * 128] for group in range(GROUPS)]
    square = groups[0] * groups[0]
    for values in groups[1:]:
        square = square + values * values
    scale = lax.rsqrt(jnp.sum(square, axis=1, keepdims=True) + 1e-06)
    tops = [
        jnp.log2(jnp.maximum(jnp.max(jnp.abs(values), axis=1, keepdims=True), TINY))
        for values in groups
    ]
    top = tops[0]
    for other in tops[1:]:
        top = jnp.maximum(top, other)
    power = jnp.clip(jnp.ceil(top * 32.0), LEAST_POWER, 4096.0)
    top = power * (1.0 / 32.0)
    factor = jnp.where(scale > 0.0, top - 15.0 + jnp.log2(jnp.maximum(scale, TINY)), -250.0)
    coarse = jnp.round(factor * 128.0)
    fine = jnp.round((factor - coarse * (1.0 / 128.0)) * FINE)
    fields = jnp.where(second == POWER, power, 0.0)
    fields = jnp.where(second == COARSE, coarse, jnp.where(second == COARSE + 1, fine, fields))
    for group, values in enumerate(groups):
        below = jnp.clip(jnp.floor(top - tops[group]), 0.0, 30.0)
        steps = jnp.round(values * jnp.exp2(15.0 - top + below))
        here = slice(group * 128, (group + 1) * 128)
        sent_ref[:, here] = stored(*placed(jnp.clip(steps, -32767.0, 32767.0)))
        fields = jnp.where(second == CLUS_DEV + group, below, fields)
    labels = (first == label).astype(jnp.bfloat16)
    high, low = placed(fields)
    sent_ref[:, DIM:] = stored(high, low + product(chosen, labels, ((1,), (1,))))


def fields_of(ref, here):
    tail = ref[here, DIM:].astype(jnp.float32)
    lane = iota(tail.shape, 1)
    member = jnp.where(lane < CLUS_DEV, tail, 0.0).astype(jnp.bfloat16)
    group = (lane >= CLUS_DEV) & (lane < CLUS_DEV + GROUPS)
    below = jnp.where(group, jnp.exp2(-jnp.where(group, tail, 0.0)), 0.0).astype(jnp.bfloat16)
    spread = iota((128, DIM), 1) // 128 + CLUS_DEV == iota((128, DIM), 0)
    return tail, member, product(below, spread.astype(jnp.bfloat16), ((1,), (0,)))


def score_kernel(all_ref, best_ref, unit_ref, member_ref):
    for start in range(0, all_ref.shape[0], HALF):
        here = slice(start, start + HALF)
        tail, member, below = fields_of(all_ref, here)
        factor = jnp.exp2(
            tail[:, COARSE : COARSE + 1] * (1.0 / 128.0)
            + tail[:, COARSE + 1 : COARSE + 2] * (1.0 / FINE)
        )
        unit_ref[here, :] = (all_ref[here, :DIM].astype(jnp.float32) * (below * factor)).astype(
            jnp.bfloat16
        )
        member_ref[here, :] = member
    place = lax.axis_index("yl") * 2 + lax.axis_index("core")
    offset = pl.multiple_of(place * SLOTS, SLOTS)
    own = unit_ref[pl.ds(offset, SLOTS), :]
    own_member = member_ref[pl.ds(offset, SLOTS), :]
    apart = iota((SLOTS, SLOTS), 1) - iota((SLOTS, SLOTS), 0) + offset
    best = jnp.full((SLOTS, SLOTS), -1.0, jnp.float32)
    for start in range(0, all_ref.shape[0], SLOTS):
        here = slice(start, start + SLOTS)
        scores = product(unit_ref[here, :], own, ((1,), (1,)))
        same = product(member_ref[here, :], own_member, ((1,), (1,))) > 0.5
        best = jnp.maximum(best, jnp.where(same & (apart != start), scores, -1.0))
    most = jnp.max(best, axis=0, keepdims=True)
    slot_of = iota((OWNERS, SLOTS), 1) - iota((OWNERS, SLOTS), 0) * 2
    first, second = [
        jnp.sum(jnp.where(slot_of == slot, most, 0.0), axis=1, keepdims=True) for slot in range(2)
    ]
    best_ref[...] = jnp.where(iota((OWNERS, 128), 1) < 64, first, second)


def centroid_kernel(all_ref, centroid_ref):
    sums = jnp.zeros((CLUS_DEV, DIM), jnp.float32)
    for start in range(0, all_ref.shape[0], SLOTS):
        here = slice(start, start + SLOTS)
        tail, member, below = fields_of(all_ref, here)
        step = jnp.exp2(tail[:, POWER : POWER + 1] * (1.0 / 32.0) - 15.0)
        rows = all_ref[here, :DIM].astype(jnp.float32) * (below * step)
        for piece in pieces(rows):
            sums = sums + product(member, piece, ((0,), (0,)))[:CLUS_DEV]
    centroid_ref[...] = sums * lax.rsqrt(jnp.sum(sums * sums, axis=1, keepdims=True) + 1e-06)


def choose_kernel(made_ref, other_ref, centroid_ref):
    mine = lax.axis_index("yh") == lax.axis_index("core")
    centroid_ref[...] = jnp.where(mine, made_ref[...], other_ref[...])


def pick_kernel(returned_ref, code_ref, nearest_ref):
    code = code_ref[...]
    owner = code // 2
    first_slot = code == owner * 2
    values = jnp.where(first_slot, returned_ref[:, :1], returned_ref[:, 127:])
    mine = iota((OWNERS, ROWS), 0) == owner
    nearest_ref[...] = jnp.sum(jnp.where(mine, values, 0.0), axis=0, keepdims=True)


def call(kernel, outs, *operands, scratch=()):
    spec = pl.BlockSpec(memory_space=pltpu.VMEM)
    many = isinstance(outs, list)
    return pl.pallas_call(
        kernel,
        out_shape=outs,
        in_specs=[spec] * len(operands),
        out_specs=[spec] * len(outs) if many else spec,
        scratch_shapes=scratch,
        compiler_params=VMEM,
    )(*operands)


def exchange(value):
    return lax.all_to_all(value, OWNER_AXES, split_axis=0, concat_axis=0, tiled=True)


def on_device(embeddings, cluster):
    shape = jax.ShapeDtypeStruct
    sent, code = call(
        place_kernel,
        [shape((SLOTS, WIDE), jnp.int16), shape((1, ROWS), jnp.int32)],
        embeddings,
        cluster.reshape(1, ROWS),
    )
    rows = lax.all_gather(exchange(sent), MEET_AXES, axis=0, tiled=True)
    best = call(
        score_kernel,
        shape((OWNERS, 128), jnp.float32),
        rows,
        scratch=[
            pltpu.VMEM((rows.shape[0], DIM), jnp.bfloat16),
            pltpu.VMEM((rows.shape[0], 128), jnp.bfloat16),
        ],
    )
    returned = exchange(best)
    made = call(centroid_kernel, shape((CLUS_DEV, DIM), jnp.float32), rows)
    other = lax.ppermute(made, "yh", [(0, 1), (1, 0)])
    centroids = call(choose_kernel, shape((CLUS_DEV, DIM), jnp.float32), made, other)
    nearest = call(pick_kernel, shape((1, ROWS), jnp.float32), returned, code)
    return centroids, nearest.reshape(ROWS)


def solution(mesh):
    split = tuple(AXES)
    return jax.shard_map(
        on_device,
        mesh=Mesh(mesh.devices.reshape(tuple(AXES.values())), split),
        in_specs=(P(split, None), P(split)),
        out_specs=(P(("z", "x", "core"), None), P(split)),
        check_vma=False,
    )
```

```python
import jax
import jax.numpy as jnp
from jax import lax
from jax.experimental import pallas as pl
from jax.experimental.pallas import tpu as pltpu
from jax.sharding import Mesh
from jax.sharding import PartitionSpec as P

CLUS_DEV = 8
AXES = {"z": 16, "xh": 2, "xl": 2, "core": 2, "y": 4}
OWNER_AXES = ("z", "xh", "y")
MEET_AXES = ("xl", "core")
OWNERS = 128
ROWS = 128
SLOTS = 256
DIM = 768
WIDE = DIM + 128
GROUPS = DIM // 128
HALF = 512
LEAST_POWER = -2560.0
COARSE = CLUS_DEV + GROUPS
POWER = COARSE + 2
FINE = 2.0**21
TINY = 1e-37
EDGE = 3.38e38
VMEM = pltpu.CompilerParams(vmem_limit_bytes=48 * 1024 * 1024)


def narrow(value):
    return jnp.clip(value, -EDGE, EDGE).astype(jnp.bfloat16)


def pieces(value):
    high = narrow(value)
    rest = value - high.astype(jnp.float32)
    middle = rest.astype(jnp.bfloat16)
    low = (rest - middle.astype(jnp.float32)).astype(jnp.bfloat16)
    return high, middle, low


def product(left, right, contract):
    return lax.dot_general(
        left, right, (contract, ((), ())), preferred_element_type=jnp.float32
    )


def iota(shape, dimension):
    return lax.broadcasted_iota(jnp.int32, shape, dimension)


def stored(high, low):
    return (high * 256.0 + low).astype(jnp.int32).astype(jnp.int16)


def place_kernel(rows_ref, cluster_ref, sent_ref, code_ref):
    cluster = cluster_ref[...]
    owner = cluster // CLUS_DEV
    label = cluster - owner * CLUS_DEV
    first = iota((OWNERS, ROWS), 0)
    second = iota((OWNERS, ROWS), 1)
    hits = first == owner
    earlier = product(
        hits.astype(jnp.bfloat16), (first < second).astype(jnp.bfloat16), ((1,), (0,))
    )
    position = jnp.sum(jnp.where(hits & (earlier > 0.5), 1, 0), axis=0, keepdims=True)
    code = owner * 2 + position
    code_ref[...] = code
    chosen = (iota((SLOTS, ROWS), 0) == code).astype(jnp.bfloat16)

    def placed(steps):
        high = jnp.floor(steps * (1.0 / 256.0) + 0.5)
        low = steps - high * 256.0
        return (
            product(chosen, high.astype(jnp.bfloat16), ((1,), (0,))),
            product(chosen, low.astype(jnp.bfloat16), ((1,), (0,))),
        )

    groups = [rows_ref[:, group * 128 : (group + 1) * 128] for group in range(GROUPS)]
    square = groups[0] * groups[0]
    for values in groups[1:]:
        square = square + values * values
    scale = lax.rsqrt(jnp.sum(square, axis=1, keepdims=True) + 1e-06)
    tops = [
        jnp.log2(jnp.maximum(jnp.max(jnp.abs(values), axis=1, keepdims=True), TINY))
        for values in groups
    ]
    top = tops[0]
    for other in tops[1:]:
        top = jnp.maximum(top, other)
    power = jnp.clip(jnp.ceil(top * 32.0), LEAST_POWER, 4096.0)
    top = power * (1.0 / 32.0)
    factor = jnp.where(scale > 0.0, top - 15.0 + jnp.log2(jnp.maximum(scale, TINY)), -250.0)
    coarse = jnp.round(factor * 128.0)
    fine = jnp.round((factor - coarse * (1.0 / 128.0)) * FINE)
    fields = jnp.where(second == POWER, power, 0.0)
    fields = jnp.where(second == COARSE, coarse, jnp.where(second == COARSE + 1, fine, fields))
    for group, values in enumerate(groups):
        below = jnp.clip(jnp.floor(top - tops[group]), 0.0, 30.0)
        steps = jnp.round(values * jnp.exp2(15.0 - top + below))
        here = slice(group * 128, (group + 1) * 128)
        sent_ref[:, here] = stored(*placed(jnp.clip(steps, -32767.0, 32767.0)))
        fields = jnp.where(second == CLUS_DEV + group, below, fields)
    labels = (first == label).astype(jnp.bfloat16)
    high, low = placed(fields)
    sent_ref[:, DIM:] = stored(high, low + product(chosen, labels, ((1,), (1,))))


def fields_of(ref, here):
    tail = ref[here, DIM:].astype(jnp.float32)
    lane = iota(tail.shape, 1)
    member = jnp.where(lane < CLUS_DEV, tail, 0.0).astype(jnp.bfloat16)
    group = (lane >= CLUS_DEV) & (lane < CLUS_DEV + GROUPS)
    below = jnp.where(group, jnp.exp2(-jnp.where(group, tail, 0.0)), 0.0).astype(jnp.bfloat16)
    spread = iota((128, DIM), 1) // 128 + CLUS_DEV == iota((128, DIM), 0)
    return tail, member, product(below, spread.astype(jnp.bfloat16), ((1,), (0,)))


def score_kernel(all_ref, best_ref, unit_ref, member_ref):
    for start in range(0, all_ref.shape[0], HALF):
        here = slice(start, start + HALF)
        tail, member, below = fields_of(all_ref, here)
        factor = jnp.exp2(
            tail[:, COARSE : COARSE + 1] * (1.0 / 128.0)
            + tail[:, COARSE + 1 : COARSE + 2] * (1.0 / FINE)
        )
        unit_ref[here, :] = (all_ref[here, :DIM].astype(jnp.float32) * (below * factor)).astype(
            jnp.bfloat16
        )
        member_ref[here, :] = member
    place = lax.axis_index("xl") * 2 + lax.axis_index("core")
    offset = pl.multiple_of(place * SLOTS, SLOTS)
    own = unit_ref[pl.ds(offset, SLOTS), :]
    own_member = member_ref[pl.ds(offset, SLOTS), :]
    apart = iota((SLOTS, SLOTS), 1) - iota((SLOTS, SLOTS), 0) + offset
    best = jnp.full((SLOTS, SLOTS), -1.0, jnp.float32)
    for start in range(0, all_ref.shape[0], SLOTS):
        here = slice(start, start + SLOTS)
        scores = product(unit_ref[here, :], own, ((1,), (1,)))
        same = product(member_ref[here, :], own_member, ((1,), (1,))) > 0.5
        best = jnp.maximum(best, jnp.where(same & (apart != start), scores, -1.0))
    most = jnp.max(best, axis=0, keepdims=True)
    slot_of = iota((OWNERS, SLOTS), 1) - iota((OWNERS, SLOTS), 0) * 2
    first, second = [
        jnp.sum(jnp.where(slot_of == slot, most, 0.0), axis=1, keepdims=True) for slot in range(2)
    ]
    best_ref[...] = jnp.where(iota((OWNERS, 128), 1) < 64, first, second)


def centroid_kernel(all_ref, centroid_ref):
    sums = jnp.zeros((CLUS_DEV, DIM), jnp.float32)
    for start in range(0, all_ref.shape[0], SLOTS):
        here = slice(start, start + SLOTS)
        tail, member, below = fields_of(all_ref, here)
        step = jnp.exp2(tail[:, POWER : POWER + 1] * (1.0 / 32.0) - 15.0)
        rows = all_ref[here, :DIM].astype(jnp.float32) * (below * step)
        for piece in pieces(rows):
            sums = sums + product(member, piece, ((0,), (0,)))[:CLUS_DEV]
    centroid_ref[...] = sums * lax.rsqrt(jnp.sum(sums * sums, axis=1, keepdims=True) + 1e-06)


def choose_kernel(made_ref, centroid_ref):
    place = lax.axis_index("xl") * 2 + lax.axis_index("core")
    start = pl.multiple_of(place * CLUS_DEV, CLUS_DEV)
    centroid_ref[...] = made_ref[pl.ds(start, CLUS_DEV), :]


def pick_kernel(returned_ref, code_ref, nearest_ref):
    code = code_ref[...]
    owner = code // 2
    first_slot = code == owner * 2
    values = jnp.where(first_slot, returned_ref[:, :1], returned_ref[:, 127:])
    mine = iota((OWNERS, ROWS), 0) == owner
    nearest_ref[...] = jnp.sum(jnp.where(mine, values, 0.0), axis=0, keepdims=True)


def call(kernel, outs, *operands, scratch=()):
    spec = pl.BlockSpec(memory_space=pltpu.VMEM)
    many = isinstance(outs, list)
    return pl.pallas_call(
        kernel,
        out_shape=outs,
        in_specs=[spec] * len(operands),
        out_specs=[spec] * len(outs) if many else spec,
        scratch_shapes=scratch,
        compiler_params=VMEM,
    )(*operands)


def exchange(value):
    return lax.all_to_all(value, OWNER_AXES, split_axis=0, concat_axis=0, tiled=True)


def on_device(embeddings, cluster):
    shape = jax.ShapeDtypeStruct
    sent, code = call(
        place_kernel,
        [shape((SLOTS, WIDE), jnp.int16), shape((1, ROWS), jnp.int32)],
        embeddings,
        cluster.reshape(1, ROWS),
    )
    rows = lax.all_gather(exchange(sent), MEET_AXES, axis=0, tiled=True)
    best = call(
        score_kernel,
        shape((OWNERS, 128), jnp.float32),
        rows,
        scratch=[
            pltpu.VMEM((rows.shape[0], DIM), jnp.bfloat16),
            pltpu.VMEM((rows.shape[0], 128), jnp.bfloat16),
        ],
    )
    returned = exchange(best)
    made = call(centroid_kernel, shape((CLUS_DEV, DIM), jnp.float32), rows)
    made = lax.all_gather(made, "y", axis=0, tiled=True)
    centroids = call(choose_kernel, shape((CLUS_DEV, DIM), jnp.float32), made)
    nearest = call(pick_kernel, shape((1, ROWS), jnp.float32), returned, code)
    return centroids, nearest.reshape(ROWS)


def solution(mesh):
    split = tuple(AXES)
    return jax.shard_map(
        on_device,
        mesh=Mesh(mesh.devices.reshape(tuple(AXES.values())), split),
        in_specs=(P(split, None), P(split)),
        out_specs=(P(("z", "xh", "xl", "core"), None), P(split)),
        check_vma=False,
    )
```

```python
import jax
import jax.numpy as jnp
from jax import lax
from jax.experimental import pallas as pl
from jax.experimental.pallas import tpu as pltpu
from jax.sharding import Mesh
from jax.sharding import PartitionSpec as P

CLUS_DEV = 8
AXES = {"z": 16, "x": 4, "core": 2, "yh": 2, "yl": 2}
OWNER_AXES = ("z", "x", "yh")
MEET_AXES = ("yl", "core")
OWNERS = 128
ROWS = 128
SLOTS = 256
DIM = 768
WIDE = DIM + 128
GROUPS = DIM // 128
HALF = 512
LEAST_POWER = -2560.0
COARSE = CLUS_DEV + GROUPS
POWER = COARSE + 2
FINE = 2.0**21
TINY = 1e-37
EDGE = 3.38e38
VMEM = pltpu.CompilerParams(vmem_limit_bytes=48 * 1024 * 1024)


def narrow(value):
    return jnp.clip(value, -EDGE, EDGE).astype(jnp.bfloat16)


def pieces(value):
    high = narrow(value)
    rest = value - high.astype(jnp.float32)
    middle = rest.astype(jnp.bfloat16)
    low = (rest - middle.astype(jnp.float32)).astype(jnp.bfloat16)
    return high, middle, low


def product(left, right, contract):
    return lax.dot_general(
        left, right, (contract, ((), ())), preferred_element_type=jnp.float32
    )


def iota(shape, dimension):
    return lax.broadcasted_iota(jnp.int32, shape, dimension)


def stored(high, low):
    return (high * 256.0 + low).astype(jnp.int32).astype(jnp.int16)


def place_kernel(rows_ref, cluster_ref, sent_ref, code_ref):
    cluster = cluster_ref[...]
    owner = cluster // CLUS_DEV
    label = cluster - owner * CLUS_DEV
    first = iota((OWNERS, ROWS), 0)
    second = iota((OWNERS, ROWS), 1)
    hits = first == owner
    earlier = product(
        hits.astype(jnp.bfloat16), (first < second).astype(jnp.bfloat16), ((1,), (0,))
    )
    position = jnp.sum(jnp.where(hits & (earlier > 0.5), 1, 0), axis=0, keepdims=True)
    code = owner * 2 + position
    code_ref[...] = code
    chosen = (iota((SLOTS, ROWS), 0) == code).astype(jnp.bfloat16)

    def placed(steps):
        high = jnp.floor(steps * (1.0 / 256.0) + 0.5)
        low = steps - high * 256.0
        return (
            product(chosen, high.astype(jnp.bfloat16), ((1,), (0,))),
            product(chosen, low.astype(jnp.bfloat16), ((1,), (0,))),
        )

    groups = [rows_ref[:, group * 128 : (group + 1) * 128] for group in range(GROUPS)]
    square = groups[0] * groups[0]
    for values in groups[1:]:
        square = square + values * values
    scale = lax.rsqrt(jnp.sum(square, axis=1, keepdims=True) + 1e-06)
    tops = [
        jnp.log2(jnp.maximum(jnp.max(jnp.abs(values), axis=1, keepdims=True), TINY))
        for values in groups
    ]
    top = tops[0]
    for other in tops[1:]:
        top = jnp.maximum(top, other)
    power = jnp.clip(jnp.ceil(top * 32.0), LEAST_POWER, 4096.0)
    top = power * (1.0 / 32.0)
    factor = jnp.where(scale > 0.0, top - 15.0 + jnp.log2(jnp.maximum(scale, TINY)), -250.0)
    coarse = jnp.round(factor * 128.0)
    fine = jnp.round((factor - coarse * (1.0 / 128.0)) * FINE)
    fields = jnp.where(second == POWER, power, 0.0)
    fields = jnp.where(second == COARSE, coarse, jnp.where(second == COARSE + 1, fine, fields))
    columns = []
    for group, values in enumerate(groups):
        below = jnp.clip(jnp.floor(top - tops[group]), 0.0, 30.0)
        steps = jnp.round(values * jnp.exp2(15.0 - top + below))
        columns.append(jnp.clip(steps, -32767.0, 32767.0))
        fields = jnp.where(second == CLUS_DEV + group, below, fields)
    labels = (first == label).astype(jnp.bfloat16)
    high, low = placed(jnp.concatenate(columns + [fields], axis=1))
    sent_ref[:, :DIM] = stored(high[:, :DIM], low[:, :DIM])
    sent_ref[:, DIM:] = stored(
        high[:, DIM:], low[:, DIM:] + product(chosen, labels, ((1,), (1,)))
    )


def fields_of(ref, here):
    tail = ref[here, DIM:].astype(jnp.float32)
    lane = iota(tail.shape, 1)
    member = jnp.where(lane < CLUS_DEV, tail, 0.0).astype(jnp.bfloat16)
    group = (lane >= CLUS_DEV) & (lane < CLUS_DEV + GROUPS)
    below = jnp.where(group, jnp.exp2(-jnp.where(group, tail, 0.0)), 0.0).astype(jnp.bfloat16)
    spread = iota((128, DIM), 1) // 128 + CLUS_DEV == iota((128, DIM), 0)
    return tail, member, product(below, spread.astype(jnp.bfloat16), ((1,), (0,)))


def score_kernel(all_ref, best_ref, unit_ref, member_ref):
    for start in range(0, all_ref.shape[0], HALF):
        here = slice(start, start + HALF)
        tail, member, below = fields_of(all_ref, here)
        factor = jnp.exp2(
            tail[:, COARSE : COARSE + 1] * (1.0 / 128.0)
            + tail[:, COARSE + 1 : COARSE + 2] * (1.0 / FINE)
        )
        unit_ref[here, :] = (all_ref[here, :DIM].astype(jnp.float32) * (below * factor)).astype(
            jnp.bfloat16
        )
        member_ref[here, :] = member
    place = lax.axis_index("yl") * 2 + lax.axis_index("core")
    offset = pl.multiple_of(place * SLOTS, SLOTS)
    own = unit_ref[pl.ds(offset, SLOTS), :]
    own_member = member_ref[pl.ds(offset, SLOTS), :]
    apart = iota((SLOTS, SLOTS), 1) - iota((SLOTS, SLOTS), 0) + offset
    best = jnp.full((SLOTS, SLOTS), -1.0, jnp.float32)
    for start in range(0, all_ref.shape[0], SLOTS):
        here = slice(start, start + SLOTS)
        scores = product(unit_ref[here, :], own, ((1,), (1,)))
        same = product(member_ref[here, :], own_member, ((1,), (1,))) > 0.5
        best = jnp.maximum(best, jnp.where(same & (apart != start), scores, -1.0))
    most = jnp.max(best, axis=0, keepdims=True)
    slot_of = iota((OWNERS, SLOTS), 1) - iota((OWNERS, SLOTS), 0) * 2
    first, second = [
        jnp.sum(jnp.where(slot_of == slot, most, 0.0), axis=1, keepdims=True) for slot in range(2)
    ]
    best_ref[...] = jnp.where(iota((OWNERS, 128), 1) < 64, first, second)


def centroid_kernel(all_ref, centroid_ref):
    sums = jnp.zeros((CLUS_DEV, DIM), jnp.float32)
    for start in range(0, all_ref.shape[0], SLOTS):
        here = slice(start, start + SLOTS)
        tail, member, below = fields_of(all_ref, here)
        step = jnp.exp2(tail[:, POWER : POWER + 1] * (1.0 / 32.0) - 15.0)
        rows = all_ref[here, :DIM].astype(jnp.float32) * (below * step)
        for piece in pieces(rows):
            sums = sums + product(member, piece, ((0,), (0,)))[:CLUS_DEV]
    centroid_ref[...] = sums * lax.rsqrt(jnp.sum(sums * sums, axis=1, keepdims=True) + 1e-06)


def choose_kernel(made_ref, other_ref, centroid_ref):
    mine = lax.axis_index("yh") == lax.axis_index("core")
    centroid_ref[...] = jnp.where(mine, made_ref[...], other_ref[...])


def pick_kernel(returned_ref, code_ref, nearest_ref):
    code = code_ref[...]
    owner = code // 2
    first_slot = code == owner * 2
    values = jnp.where(first_slot, returned_ref[:, :1], returned_ref[:, 127:])
    mine = iota((OWNERS, ROWS), 0) == owner
    nearest_ref[...] = jnp.sum(jnp.where(mine, values, 0.0), axis=0, keepdims=True)


def call(kernel, outs, *operands, scratch=()):
    spec = pl.BlockSpec(memory_space=pltpu.VMEM)
    many = isinstance(outs, list)
    return pl.pallas_call(
        kernel,
        out_shape=outs,
        in_specs=[spec] * len(operands),
        out_specs=[spec] * len(outs) if many else spec,
        scratch_shapes=scratch,
        compiler_params=VMEM,
    )(*operands)


def exchange(value):
    return lax.all_to_all(value, OWNER_AXES, split_axis=0, concat_axis=0, tiled=True)


def on_device(embeddings, cluster):
    shape = jax.ShapeDtypeStruct
    sent, code = call(
        place_kernel,
        [shape((SLOTS, WIDE), jnp.int16), shape((1, ROWS), jnp.int32)],
        embeddings,
        cluster.reshape(1, ROWS),
    )
    rows = lax.all_gather(exchange(sent), MEET_AXES, axis=0, tiled=True)
    best = call(
        score_kernel,
        shape((OWNERS, 128), jnp.float32),
        rows,
        scratch=[
            pltpu.VMEM((rows.shape[0], DIM), jnp.bfloat16),
            pltpu.VMEM((rows.shape[0], 128), jnp.bfloat16),
        ],
    )
    returned = exchange(best)
    made = call(centroid_kernel, shape((CLUS_DEV, DIM), jnp.float32), rows)
    other = lax.ppermute(made, "yh", [(0, 1), (1, 0)])
    centroids = call(choose_kernel, shape((CLUS_DEV, DIM), jnp.float32), made, other)
    nearest = call(pick_kernel, shape((1, ROWS), jnp.float32), returned, code)
    return centroids, nearest.reshape(ROWS)


def solution(mesh):
    split = tuple(AXES)
    return jax.shard_map(
        on_device,
        mesh=Mesh(mesh.devices.reshape(tuple(AXES.values())), split),
        in_specs=(P(split, None), P(split)),
        out_specs=(P(("z", "x", "core"), None), P(split)),
        check_vma=False,
    )
```

```python
import jax
import jax.numpy as jnp
from jax import lax
from jax.experimental import pallas as pl
from jax.experimental.pallas import tpu as pltpu
from jax.sharding import Mesh
from jax.sharding import PartitionSpec as P

CLUS_DEV = 8
AXES = {"z": 16, "x": 4, "core": 2, "yh": 2, "yl": 2}
OWNER_AXES = ("z", "x", "yh")
MEET_AXES = ("yl", "core")
OWNERS = 128
ROWS = 128
SLOTS = 256
DIM = 768
WIDE = DIM + 128
GROUPS = DIM // 128
HALF = 1024
LEAST_POWER = -2560.0
COARSE = CLUS_DEV + GROUPS
POWER = COARSE + 2
FINE = 2.0**21
TINY = 1e-37
EDGE = 3.38e38
VMEM = pltpu.CompilerParams(vmem_limit_bytes=48 * 1024 * 1024)


def narrow(value):
    return jnp.clip(value, -EDGE, EDGE).astype(jnp.bfloat16)


def pieces(value):
    high = narrow(value)
    rest = value - high.astype(jnp.float32)
    middle = rest.astype(jnp.bfloat16)
    low = (rest - middle.astype(jnp.float32)).astype(jnp.bfloat16)
    return high, middle, low


def product(left, right, contract):
    return lax.dot_general(
        left, right, (contract, ((), ())), preferred_element_type=jnp.float32
    )


def iota(shape, dimension):
    return lax.broadcasted_iota(jnp.int32, shape, dimension)


def stored(high, low):
    return (high * 256.0 + low).astype(jnp.int32).astype(jnp.int16)


def place_kernel(rows_ref, cluster_ref, sent_ref, code_ref):
    cluster = cluster_ref[...]
    owner = cluster // CLUS_DEV
    label = cluster - owner * CLUS_DEV
    first = iota((OWNERS, ROWS), 0)
    second = iota((OWNERS, ROWS), 1)
    hits = first == owner
    earlier = product(
        hits.astype(jnp.bfloat16), (first < second).astype(jnp.bfloat16), ((1,), (0,))
    )
    position = jnp.sum(jnp.where(hits & (earlier > 0.5), 1, 0), axis=0, keepdims=True)
    code = owner * 2 + position
    code_ref[...] = code
    chosen = (iota((SLOTS, ROWS), 0) == code).astype(jnp.bfloat16)

    def placed(steps):
        high = jnp.floor(steps * (1.0 / 256.0) + 0.5)
        low = steps - high * 256.0
        return (
            product(chosen, high.astype(jnp.bfloat16), ((1,), (0,))),
            product(chosen, low.astype(jnp.bfloat16), ((1,), (0,))),
        )

    groups = [rows_ref[:, group * 128 : (group + 1) * 128] for group in range(GROUPS)]
    square = groups[0] * groups[0]
    for values in groups[1:]:
        square = square + values * values
    scale = lax.rsqrt(jnp.sum(square, axis=1, keepdims=True) + 1e-06)
    tops = [
        jnp.log2(jnp.maximum(jnp.max(jnp.abs(values), axis=1, keepdims=True), TINY))
        for values in groups
    ]
    top = tops[0]
    for other in tops[1:]:
        top = jnp.maximum(top, other)
    power = jnp.clip(jnp.ceil(top * 32.0), LEAST_POWER, 4096.0)
    top = power * (1.0 / 32.0)
    factor = jnp.where(scale > 0.0, top - 15.0 + jnp.log2(jnp.maximum(scale, TINY)), -250.0)
    coarse = jnp.round(factor * 128.0)
    fine = jnp.round((factor - coarse * (1.0 / 128.0)) * FINE)
    fields = jnp.where(second == POWER, power, 0.0)
    fields = jnp.where(second == COARSE, coarse, jnp.where(second == COARSE + 1, fine, fields))
    for group, values in enumerate(groups):
        below = jnp.clip(jnp.floor(top - tops[group]), 0.0, 30.0)
        steps = jnp.round(values * jnp.exp2(15.0 - top + below))
        here = slice(group * 128, (group + 1) * 128)
        sent_ref[:, here] = stored(*placed(jnp.clip(steps, -32767.0, 32767.0)))
        fields = jnp.where(second == CLUS_DEV + group, below, fields)
    labels = (first == label).astype(jnp.bfloat16)
    high, low = placed(fields)
    sent_ref[:, DIM:] = stored(high, low + product(chosen, labels, ((1,), (1,))))


def fields_of(ref, here):
    tail = ref[here, DIM:].astype(jnp.float32)
    lane = iota(tail.shape, 1)
    member = jnp.where(lane < CLUS_DEV, tail, 0.0).astype(jnp.bfloat16)
    group = (lane >= CLUS_DEV) & (lane < CLUS_DEV + GROUPS)
    below = jnp.where(group, jnp.exp2(-jnp.where(group, tail, 0.0)), 0.0).astype(jnp.bfloat16)
    spread = iota((128, DIM), 1) // 128 + CLUS_DEV == iota((128, DIM), 0)
    return tail, member, product(below, spread.astype(jnp.bfloat16), ((1,), (0,)))


def score_kernel(all_ref, best_ref, unit_ref, member_ref):
    for start in range(0, all_ref.shape[0], HALF):
        here = slice(start, start + HALF)
        tail, member, below = fields_of(all_ref, here)
        factor = jnp.exp2(
            tail[:, COARSE : COARSE + 1] * (1.0 / 128.0)
            + tail[:, COARSE + 1 : COARSE + 2] * (1.0 / FINE)
        )
        unit_ref[here, :] = (all_ref[here, :DIM].astype(jnp.float32) * (below * factor)).astype(
            jnp.bfloat16
        )
        member_ref[here, :] = member
    place = lax.axis_index("yl") * 2 + lax.axis_index("core")
    offset = pl.multiple_of(place * SLOTS, SLOTS)
    own = unit_ref[pl.ds(offset, SLOTS), :]
    own_member = member_ref[pl.ds(offset, SLOTS), :]
    apart = iota((SLOTS, SLOTS), 1) - iota((SLOTS, SLOTS), 0) + offset
    best = jnp.full((SLOTS, SLOTS), -1.0, jnp.float32)
    for start in range(0, all_ref.shape[0], SLOTS):
        here = slice(start, start + SLOTS)
        scores = product(unit_ref[here, :], own, ((1,), (1,)))
        same = product(member_ref[here, :], own_member, ((1,), (1,))) > 0.5
        best = jnp.maximum(best, jnp.where(same & (apart != start), scores, -1.0))
    most = jnp.max(best, axis=0, keepdims=True)
    slot_of = iota((OWNERS, SLOTS), 1) - iota((OWNERS, SLOTS), 0) * 2
    first, second = [
        jnp.sum(jnp.where(slot_of == slot, most, 0.0), axis=1, keepdims=True) for slot in range(2)
    ]
    best_ref[...] = jnp.where(iota((OWNERS, 128), 1) < 64, first, second)


def centroid_kernel(all_ref, centroid_ref):
    sums = jnp.zeros((CLUS_DEV, DIM), jnp.float32)
    for start in range(0, all_ref.shape[0], SLOTS):
        here = slice(start, start + SLOTS)
        tail, member, below = fields_of(all_ref, here)
        step = jnp.exp2(tail[:, POWER : POWER + 1] * (1.0 / 32.0) - 15.0)
        rows = all_ref[here, :DIM].astype(jnp.float32) * (below * step)
        for piece in pieces(rows):
            sums = sums + product(member, piece, ((0,), (0,)))[:CLUS_DEV]
    centroid_ref[...] = sums * lax.rsqrt(jnp.sum(sums * sums, axis=1, keepdims=True) + 1e-06)


def choose_kernel(made_ref, other_ref, centroid_ref):
    mine = lax.axis_index("yh") == lax.axis_index("core")
    centroid_ref[...] = jnp.where(mine, made_ref[...], other_ref[...])


def pick_kernel(returned_ref, code_ref, nearest_ref):
    code = code_ref[...]
    owner = code // 2
    first_slot = code == owner * 2
    values = jnp.where(first_slot, returned_ref[:, :1], returned_ref[:, 127:])
    mine = iota((OWNERS, ROWS), 0) == owner
    nearest_ref[...] = jnp.sum(jnp.where(mine, values, 0.0), axis=0, keepdims=True)


def call(kernel, outs, *operands, scratch=()):
    spec = pl.BlockSpec(memory_space=pltpu.VMEM)
    many = isinstance(outs, list)
    return pl.pallas_call(
        kernel,
        out_shape=outs,
        in_specs=[spec] * len(operands),
        out_specs=[spec] * len(outs) if many else spec,
        scratch_shapes=scratch,
        compiler_params=VMEM,
    )(*operands)


def exchange(value):
    return lax.all_to_all(value, OWNER_AXES, split_axis=0, concat_axis=0, tiled=True)


def on_device(embeddings, cluster):
    shape = jax.ShapeDtypeStruct
    sent, code = call(
        place_kernel,
        [shape((SLOTS, WIDE), jnp.int16), shape((1, ROWS), jnp.int32)],
        embeddings,
        cluster.reshape(1, ROWS),
    )
    rows = lax.all_gather(exchange(sent), MEET_AXES, axis=0, tiled=True)
    best = call(
        score_kernel,
        shape((OWNERS, 128), jnp.float32),
        rows,
        scratch=[
            pltpu.VMEM((rows.shape[0], DIM), jnp.bfloat16),
            pltpu.VMEM((rows.shape[0], 128), jnp.bfloat16),
        ],
    )
    returned = exchange(best)
    made = call(centroid_kernel, shape((CLUS_DEV, DIM), jnp.float32), rows)
    other = lax.ppermute(made, "yh", [(0, 1), (1, 0)])
    centroids = call(choose_kernel, shape((CLUS_DEV, DIM), jnp.float32), made, other)
    nearest = call(pick_kernel, shape((1, ROWS), jnp.float32), returned, code)
    return centroids, nearest.reshape(ROWS)


def solution(mesh):
    split = tuple(AXES)
    return jax.shard_map(
        on_device,
        mesh=Mesh(mesh.devices.reshape(tuple(AXES.values())), split),
        in_specs=(P(split, None), P(split)),
        out_specs=(P(("z", "x", "core"), None), P(split)),
        check_vma=False,
    )
```
